256 devices in a mesh: samples: 128 (over x_hi, y, z, core), feat: 2 (over x_lo).
Axes of the slice: x: 4 (x_hi: 2, x_lo: 2; x = x_hi * 2 + x_lo), y: 4, z: 8, core: 2. Of those that a mesh axis runs over, the one named last changes fastest.
Arguments:
- samples: float32 [32768, 4096], P('samples', 'feat'), may hold values from -12 to 12, as said below
- factor: float32 [4096, 512], P('feat'), may hold values from -6 to 6
Outputs:
- new_factor: float32 [4096, 512], P('feat')
The draws below stay inside these ranges and needn't reach their ends.
Inputs may be any that keep to these rules, and one draw needn't show every extreme that they name: `samples`: Real-valued data.
All inputs are finite; a program needn't handle non-finite values.
Results may differ from the reference program's by a relative error of at most 0.00007.
Values sent between devices are 32-bit elements; how exact they have to be, the bound alone decides.
A program may use at most 64 MiB of HBM per device.

```python
import jax
import jax.numpy as jnp
from jax import lax

D = 4096
R = 512
NROWS = 32768


def draw_samples(key, part):
    key_scale, key_main, key_skew, key_coef = jax.random.split(jax.random.fold_in(key, 11), 4)
    position = jnp.arange(D, dtype=jnp.float32) / D
    spread = jax.random.uniform(key_scale, (D,), jnp.float32)
    scales = 10.0 ** (0.5 * position + 0.5 * spread - 0.5)
    coefs = jax.random.uniform(key_coef, (D,), jnp.float32, 0.2, 0.6)
    skewed = jnp.clip(jax.random.normal(key_skew, (NROWS, D), jnp.float32), -4.0, 4.0)
    main = jnp.clip(jax.random.normal(key_main, (NROWS, D), jnp.float32), -5.0, 5.0)
    values = scales[None, :] * (main + coefs[None, :] * (skewed * skewed - 1.0))
    return jnp.clip(values, -12.0, 12.0)


def level_of(rng, shape, shards, smallest, largest):
    factor_of = 1.0
    for dim, shards_of in shards:
        steps = jax.random.uniform(jax.random.fold_in(jax.random.fold_in(rng, 6), dim), (shards_of,), jnp.float32, smallest / len(shards), largest / len(shards))
        factor_of = factor_of * jnp.repeat(jnp.exp(steps), shape[dim] // shards_of).reshape((-1,) + (1,) * (len(shape) - 1 - dim))
    return factor_of


def scatter_about(rng, extent, scale, reach, cuts=(), kind=jnp.bfloat16):
    entries = scale * jax.random.normal(rng, extent, jnp.float32)
    if cuts:
        entries = entries * level_of(rng, extent, cuts, -0.22, 0.18)
    return jnp.clip(entries, -reach, reach).astype(kind)


def setup_inputs(seed: int = 0) -> dict:
    arg_keys = jax.random.split(jax.random.key(seed), 3)
    return {
        "samples": draw_samples(jax.random.fold_in(arg_keys[2], 71), 0),
        "factor": scatter_about(arg_keys[1], (D, R), 1.0, 6.0, ((0, 2),), jnp.float32),
    }


def reference(samples, factor):
    high = lax.Precision.HIGHEST
    scaled = factor * (1.0 / jnp.sqrt(jnp.float32(D)))
    proj = jnp.dot(samples, scaled, precision=high, preferred_element_type=jnp.float32)
    squared = proj * proj
    moment = lax.dot_general(samples, squared, (((0,), (0,)), ((), ())), precision=high, preferred_element_type=jnp.float32) / NROWS
    gram = lax.dot_general(scaled, scaled, (((0,), (0,)), ((), ())), precision=high, preferred_element_type=jnp.float32)
    gram_term = jnp.dot(scaled, gram * gram, precision=high, preferred_element_type=jnp.float32)
    grad = 6.0 / jnp.sqrt(jnp.float32(D)) * (gram_term - moment)
    rms = jnp.sqrt(jnp.sum(grad * grad) / (D * R)) + 1e-06
    return factor - 0.5 * grad / rms
```

```python
import jax
import jax.numpy as jnp
from jax import lax
from jax.experimental import pallas as pl
from jax.experimental.pallas import tpu as pltpu
from jax.sharding import PartitionSpec as P

D = 4096
R = 512
NROWS = 32768
HALF = D // 2
ROWS = 256
COLS = 256
MINE = HALF // 2
MESH = pl.DeviceIdType.MESH
F32 = jnp.float32
BF16 = jnp.bfloat16

STREAMS = ((1, 0, 4), (-1, 1, 4), (1, 1, 3), (-1, 0, 3))
SLOT = {}
for _k in range(1, 5):
    for _i, (_, _, _hops) in enumerate(STREAMS):
        if _k <= _hops:
            SLOT[(_i, _k)] = len(SLOT)
NSLOT = len(SLOT)


def split(v):
    hi = v.astype(BF16)
    return hi, (v - hi.astype(F32)).astype(BF16)


def dot3(ah, al, bh, bl, dims=(((1,), (0,)), ((), ()))):
    def one(a, b):
        return lax.dot_general(a, b, dims, preferred_element_type=F32)

    return one(ah, bh) + (one(ah, bl) + one(al, bh))


def kernel(
    x_hbm, f_hbm, o_ref,
    xv, xo, fv, fh, fl, xh, xl, p, pr, s, so, xth, xtl, mom,
    ring, acc_a, dir_a, yrecv, acc_b, zrecv, acc_b2, xrecv,
    g, gr, g2, grad_a, grad_b, ss1, ss2, ss3, ss4,
    load_sem, send, recv,
):
    sidx = lax.axis_index("samples")
    feat = lax.axis_index("feat")
    core = lax.rem(sidx, 2)
    z = lax.rem(sidx // 2, 8)
    y = lax.rem(sidx // 16, 4)
    xhi = sidx // 64

    def dev(a, b, c, d, e):
        return (((a * 4 + b) * 8 + c) * 2 + d, e)

    other = dev(xhi, y, z, 1 - core, feat)
    partner = dev(xhi, y, z, core, 1 - feat)

    def yx_of(j):
        return lax.rem(y + j // 2, 4), lax.rem(xhi + j % 2, 2)

    def yx_peer(j):
        a, b = yx_of(j)
        return dev(b, a, z, core, feat)

    def z_of(j):
        return lax.rem(z + j + 8, 8)

    def z_peer(j):
        return dev(xhi, y, z_of(j), core, feat)

    counter = [0]

    def start(src, dst, to):
        i = counter[0]
        counter[0] += 1
        c = pltpu.make_async_remote_copy(
            src_ref=src, dst_ref=dst, send_sem=send.at[i], recv_sem=recv.at[i],
            device_id=to, device_id_type=MESH,
        )
        c.start()
        return c

    loads = []
    for i in range(2):
        loads.append(pltpu.make_async_copy(f_hbm.at[:, pl.ds(i * COLS, COLS)], fv.at[i], load_sem.at[i]))
    loads.append(pltpu.make_async_copy(x_hbm, xv, load_sem.at[2]))
    loads[2].start()
    loads[0].start()
    loads[1].start()
    barrier = pltpu.get_barrier_semaphore()
    everyone = [other, partner] + [yx_peer(j) for j in range(1, 8)] + [z_peer(j) for j in range(1, 8)]
    for to in everyone:
        pl.semaphore_signal(barrier, inc=1, device_id=to, device_id_type=MESH)
    loads[2].wait()

    def split_x(i, _):
        r = pl.ds(i * 32, 32)
        xh[r, :], xl[r, :] = split(xv[r, :])
        return 0

    lax.fori_loop(0, ROWS // 32, split_x, 0)

    def split_f(h):
        def body(i, _):
            r = pl.ds(pl.multiple_of(i * 128, 128), 128)
            fh[h, r, :], fl[h, r, :] = split(fv[h, r, :])
            return 0

        lax.fori_loop(0, HALF // 128, body, 0)

    def project(h):
        p[h] = jnp.zeros((ROWS, COLS), F32)

        def body(k, _):
            r = pl.ds(pl.multiple_of(k * 512, 512), 512)
            p[h] += dot3(xh[:, r], xl[:, r], fh[h, r, :], fl[h, r, :])
            return 0

        lax.fori_loop(0, HALF // 512, body, 0)


    loads[0].wait()
    split_f(0)
    project(0)
    pl.semaphore_wait(barrier, len(everyone))
    proj_copy = [start(p.at[0], pr.at[0], partner)]
    x_copy = start(x_hbm.at[:, pl.ds(pl.multiple_of((1 - core) * MINE, MINE), MINE)], xo, other)
    loads[1].wait()
    split_f(1)
    project(1)
    proj_copy.append(start(p.at[1], pr.at[1], partner))

    def turn(src, base, at):
        def body(i, _):
            c = pl.ds(pl.multiple_of(base + i * 128, 128), 128)
            r = pl.ds(pl.multiple_of(i * 128, 128), 128)
            hi, lo = split(src[:, c].T)
            xth[r, at : at + ROWS] = hi
            xtl[r, at : at + ROWS] = lo
            return 0

        lax.fori_loop(0, MINE // 128, body, 0)

    turn(xv, core * MINE, 0)
    x_copy.wait()
    turn(xo, 0, ROWS)

    contract = (((0,), (0,)), ((), ()))
    g[...] = jnp.zeros_like(g)

    def gram_body(k, _):
        r = pl.ds(pl.multiple_of(k * 512, 512), 512)
        ah, al = fh[core, r, :], fl[core, r, :]
        for h in range(2):
            g[:, h * COLS : (h + 1) * COLS] += dot3(ah, al, fh[h, r, :], fl[h, r, :], contract)
        return 0

    lax.fori_loop(0, HALF // 512, gram_body, 0)

    s_copy = []
    for h in range(2):
        proj_copy[h].wait()
        total = p[h] + pr[h]
        s[h] = total * total
        s_copy.append(start(s.at[h], so.at[h], other))
    g_copy = start(g, gr, partner)

    def moment(h):
        ah, al = split(s[h])
        bh, bl = split(so[h])
        sh = jnp.concatenate([ah, bh], axis=0)
        sl = jnp.concatenate([al, bl], axis=0)

        def body(i, _):
            r = pl.ds(pl.multiple_of(i * 256, 256), 256)
            mom[h, r, :] = dot3(xth[r, :], xtl[r, :], sh, sl)
            return 0

        lax.fori_loop(0, MINE // 256, body, 0)

    def zrows(zz, half):
        return pl.ds(pl.multiple_of(zz * 128 + half * 64, 64), 64)

    ring_copy = {}

    def ring_step(k):
        for i, (way, half, hops) in enumerate(STREAMS):
            if k > hops:
                continue
            r = zrows(z_of(way * (hops + 1 - k)), half)
            if k > 1:
                ring_copy[(i, k - 1)].wait_recv()
                mom[0, r, :] += ring[SLOT[(i, k - 1)]]
            ring_copy[(i, k)] = start(mom.at[0, r, :], ring.at[SLOT[(i, k)]], z_peer(way))

    s_copy[0].wait()
    moment(0)
    ring_step(1)
    s_copy[1].wait()
    moment(1)
    y_copy = {}
    for j in (2, 1, 3):
        yy = lax.rem(y + j, 4)
        y_copy[j] = start(
            mom.at[1, pl.ds(pl.multiple_of(yy * 256, 256), 256), :], yrecv.at[j - 1], dev(xhi, yy, z, core, feat)
        )
    ring_step(2)

    g_copy.wait()
    whole = (g[...] + gr[...]) * (1.0 / D)
    g2[core] = whole * whole
    g2_copy = start(g2.at[core], g2.at[core], other)

    ring_step(3)
    ring_step(4)

    for half in range(2):
        parts = []
        for i, (way, h, hops) in enumerate(STREAMS):
            if h == half:
                ring_copy[(i, hops)].wait_recv()
                parts.append(ring[SLOT[(i, hops)]])
        acc_a[half * 64 : half * 64 + 64, :] = mom[0, zrows(z, half), :] + (parts[0] + parts[1])
    da_copy = {}
    for j in range(1, 8):
        a, b = yx_of(j)
        r = pl.ds(pl.multiple_of(a * 32 + b * 16, 16), 16)
        da_copy[j] = start(acc_a.at[r, :], dir_a.at[j - 1], yx_peer(j))

    for j in (1, 3, 2):
        y_copy[j].wait_recv()
    acc_b[...] = (mom[1, pl.ds(pl.multiple_of(y * 256, 256), 256), :] + yrecv[0]) + (yrecv[1] + yrecv[2])
    zb_copy = {}
    for j in (4, 3, 5, 2, 6, 1, 7):
        r = pl.ds(pl.multiple_of(z_of(j) * 32, 32), 32)
        zb_copy[j] = start(acc_b.at[r, :], zrecv.at[j - 1], z_peer(j))

    g2_copy.wait()
    scale = 6.0 / 64.0

    def finish(h, at, total):
        at = pl.multiple_of(at, 16)
        term = jnp.zeros((16, COLS), F32)
        for q in range(2):
            ah, al = split(fv[q, pl.ds(at, 16), :] * (1.0 / 64.0))
            bh, bl = split(g2[q, :, h * COLS : (h + 1) * COLS])
            term += dot3(ah, al, bh, bl)
        return scale * (term - total * (1.0 / (NROWS * D)))

    row_a = core * MINE + z * 128 + y * 32 + xhi * 16
    row_b = core * MINE + y * 256 + z * 32 + xhi * 16
    own_a = acc_a[pl.ds(pl.multiple_of(y * 32 + xhi * 16, 16), 16), :]
    for j in range(1, 8):
        da_copy[j].wait_recv()
    for j in range(1, 8):
        own_a = own_a + dir_a[j - 1]
    ga = finish(0, row_a, own_a)
    mine_a = pl.ds(pl.multiple_of(row_a, 16), 16)
    grad_a[mine_a, :] = ga
    aa_copy = {}
    for j in range(1, 8):
        aa_copy[j] = start(grad_a.at[mine_a, :], grad_a.at[mine_a, :], yx_peer(j))

    for j in range(1, 8):
        zb_copy[j].wait_recv()
    own_b = acc_b[pl.ds(pl.multiple_of(z * 32, 32), 32), :]
    for j in range(1, 8):
        own_b = own_b + zrecv[j - 1]
    acc_b2[...] = own_b
    xb_copy = start(acc_b2.at[pl.ds(pl.multiple_of((1 - xhi) * 16, 16), 16), :], xrecv, yx_peer(1))

    for j in range(1, 8):
        aa_copy[j].wait_recv()
    base = core * MINE
    gather = {}
    forward = []

    def grows(zz, half):
        return pl.ds(pl.multiple_of(base + zz * 128 + half * 64, 64), 64)

    def gather_step(k):
        for i, (way, half, hops) in enumerate(STREAMS):
            if k > hops:
                continue
            r = grows(z_of(-way * (k - 1)), half)
            if k > 1:
                gather[(i, k - 1)].wait_recv()
            gather[(i, k)] = start(grad_a.at[r, :], grad_a.at[r, :], z_peer(way))
            if k > 1:
                forward.append(start(grad_a.at[r, :], grad_a.at[r, :], other))

    gather_step(1)
    r = pl.ds(pl.multiple_of(base + z * 128, 128), 128)
    forward.append(start(grad_a.at[r, :], grad_a.at[r, :], other))

    xb_copy.wait_recv()
    gb = finish(1, row_b, acc_b2[pl.ds(pl.multiple_of(xhi * 16, 16), 16), :] + xrecv[...])
    mine_b = pl.ds(pl.multiple_of(row_b, 16), 16)
    grad_b[mine_b, :] = gb
    xg_copy = start(grad_b.at[mine_b, :], grad_b.at[mine_b, :], yx_peer(1))

    sq = ga * ga + gb * gb
    tile = (sq[0:8, 0:128] + sq[8:16, 0:128]) + (sq[0:8, 128:256] + sq[8:16, 128:256])
    me1 = y * 2 + xhi
    ss1[me1] = tile
    s1_copy = [start(ss1.at[me1], ss1.at[me1], yx_peer(j)) for j in range(1, 8)]

    gather_step(2)
    xg_copy.wait_recv()
    pair = pl.ds(pl.multiple_of(base + y * 256 + z * 32, 32), 32)
    zg_copy = [start(grad_b.at[pair, :], grad_b.at[pair, :], z_peer(j)) for j in (4, 3, 5, 2, 6, 1, 7)]
    for c in s1_copy:
        c.wait_recv()
    tile = ss1[0]
    for j in range(1, 8):
        tile = tile + ss1[j]
    ss2[z] = tile
    s2_copy = [start(ss2.at[z], ss2.at[z], z_peer(j)) for j in range(1, 8)]
    gather_step(3)
    for c in zg_copy:
        c.wait_recv()
    block = pl.ds(pl.multiple_of(base + y * 256, 256), 256)
    yg_copy = {}
    for j in (2, 1, 3):
        yy = lax.rem(y + j, 4)
        yg_copy[j] = start(grad_b.at[block, :], grad_b.at[block, :], dev(xhi, yy, z, core, feat))
    forward.append(start(grad_b.at[block, :], grad_b.at[block, :], other))
    for c in s2_copy:
        c.wait_recv()
    tile = ss2[0]
    for j in range(1, 8):
        tile = tile + ss2[j]
    ss3[core] = tile
    s3_copy = start(ss3.at[core], ss3.at[core], other)
    gather_step(4)
    s3_copy.wait_recv()
    ss4[feat] = ss3[0] + ss3[1]
    s4_copy = start(ss4.at[feat], ss4.at[feat], partner)

    for i, (way, half, hops) in enumerate(STREAMS):
        gather[(i, hops)].wait_recv()
        r = grows(z_of(-way * hops), half)
        forward.append(start(grad_a.at[r, :], grad_a.at[r, :], other))
    for j in (1, 3, 2):
        yg_copy[j].wait_recv()
        r = pl.ds(pl.multiple_of(base + lax.rem(y - j + 4, 4) * 256, 256), 256)
        forward.append(start(grad_b.at[r, :], grad_b.at[r, :], other))
    s4_copy.wait_recv()
    total = jnp.sum(ss4[0] + ss4[1], keepdims=True)
    rms = jnp.sqrt(total * (1.0 / (D * R))) + 1e-06
    step = 0.5 / rms
    for c in forward:
        c.wait_recv()

    def update(i, _):
        r = pl.ds(pl.multiple_of(i * 128, 128), 128)
        o_ref[r, 0:COLS] = fv[0, r, :] - grad_a[r, :] * step
        o_ref[r, COLS:R] = fv[1, r, :] - grad_b[r, :] * step
        return 0

    lax.fori_loop(0, HALF // 128, update, 0)

    sends = list(ring_copy.values()) + list(y_copy.values()) + list(da_copy.values()) + list(zb_copy.values())
    sends += list(aa_copy.values()) + [xb_copy] + list(gather.values()) + forward + [xg_copy] + s1_copy + zg_copy
    sends += s2_copy + list(yg_copy.values()) + [s3_copy, s4_copy]
    for c in sends:
        c.wait_send()


NSEM = 160


def per_device(samples, factor):
    vm = pltpu.VMEM
    scratch = [
        vm((ROWS, HALF), F32), vm((ROWS, MINE), F32), vm((2, HALF, COLS), F32),
        vm((2, HALF, COLS), BF16), vm((2, HALF, COLS), BF16),
        vm((ROWS, HALF), BF16), vm((ROWS, HALF), BF16),
        vm((2, ROWS, COLS), F32), vm((2, ROWS, COLS), F32), vm((2, ROWS, COLS), F32), vm((2, ROWS, COLS), F32),
        vm((MINE, 2 * ROWS), BF16), vm((MINE, 2 * ROWS), BF16), vm((2, MINE, COLS), F32),
        vm((NSLOT, 64, COLS), F32), vm((128, COLS), F32), vm((7, 16, COLS), F32),
        vm((3, 256, COLS), F32), vm((256, COLS), F32), vm((7, 32, COLS), F32), vm((32, COLS), F32), vm((16, COLS), F32),
        vm((256, R), F32), vm((256, R), F32), vm((2, 256, R), F32),
        vm((HALF, COLS), F32), vm((HALF, COLS), F32),
        vm((8, 8, 128), F32), vm((8, 8, 128), F32), vm((2, 8, 128), F32), vm((2, 8, 128), F32),
        pltpu.SemaphoreType.DMA((3,)), pltpu.SemaphoreType.DMA((NSEM,)), pltpu.SemaphoreType.DMA((NSEM,)),
    ]
    return pl.pallas_call(
        kernel,
        out_shape=jax.ShapeDtypeStruct((HALF, R), F32),
        in_specs=[pl.BlockSpec(memory_space=pl.ANY)] * 2,
        out_specs=pl.BlockSpec(memory_space=pltpu.VMEM),
        scratch_shapes=scratch,
        name="cp_step",
        cost_estimate=pl.CostEstimate(flops=10**10, bytes_accessed=10**7, transcendentals=0),
        compiler_params=pltpu.CompilerParams(
            collective_id=0, has_side_effects=True, vmem_limit_bytes=50 * 2**20
        ),
    )(samples, factor)


def solution(mesh):
    placed = (P("samples", "feat"), P("feat", None))
    return jax.shard_map(
        per_device, mesh=mesh, in_specs=placed, out_specs=P("feat", None), check_vma=False
    )
```

```python
import jax
import jax.numpy as jnp
from jax import lax
from jax.experimental import pallas as pl
from jax.experimental.pallas import tpu as pltpu
from jax.sharding import PartitionSpec as P

D = 4096
R = 512
NROWS = 32768
HALF = D // 2
ROWS = 256
COLS = 256
DEPTH = 512
MINE = HALF // 2
MESH = pl.DeviceIdType.MESH
F32 = jnp.float32
BF16 = jnp.bfloat16

STREAMS = ((1, 0, 4), (-1, 1, 4), (1, 1, 3), (-1, 0, 3))
SLOT = {}
for _k in range(1, 5):
    for _i, (_, _, _hops) in enumerate(STREAMS):
        if _k <= _hops:
            SLOT[(_i, _k)] = len(SLOT)
NSLOT = len(SLOT)


def split(v):
    hi = v.astype(BF16)
    return hi, (v - hi.astype(F32)).astype(BF16)


def dot3(ah, al, bh, bl, dims=(((1,), (0,)), ((), ()))):
    def one(a, b):
        return lax.dot_general(a, b, dims, preferred_element_type=F32)

    return one(ah, bh) + (one(ah, bl) + one(al, bh))


def kernel(
    x_hbm, f_hbm, o_ref,
    xv, xo, fv, fh, fl, xh, xl, p, pr, s, so, xth, xtl, mom,
    ring, acc_a, dir_a, yrecv, acc_b, zrecv, acc_b2, xrecv,
    g, gr, g2, term, grad, ss1, ss2, ss3, ss4,
    load_sem, send, recv,
):
    sidx = lax.axis_index("samples")
    feat = lax.axis_index("feat")
    core = lax.rem(sidx, 2)
    z = lax.rem(sidx // 2, 8)
    y = lax.rem(sidx // 16, 4)
    xhi = sidx // 64

    def dev(a, b, c, d, e):
        return (((a * 4 + b) * 8 + c) * 2 + d, e)

    other = dev(xhi, y, z, 1 - core, feat)
    partner = dev(xhi, y, z, core, 1 - feat)

    def yx_of(j):
        return lax.rem(y + j // 2, 4), lax.rem(xhi + j % 2, 2)

    def yx_peer(j):
        a, b = yx_of(j)
        return dev(b, a, z, core, feat)

    def y_of(j):
        return lax.rem(y + j + 4, 4)

    def y_peer(j):
        return dev(xhi, y_of(j), z, core, feat)

    def z_of(j):
        return lax.rem(z + j + 8, 8)

    def z_peer(j):
        return dev(xhi, y, z_of(j), core, feat)

    def span(at, n):
        return pl.ds(pl.multiple_of(at, 16), n)

    counter = [0]
    unsent = []

    def start(src, dst, to):
        i = counter[0]
        counter[0] += 1
        c = pltpu.make_async_remote_copy(
            src_ref=src, dst_ref=dst, send_sem=send.at[i], recv_sem=recv.at[i],
            device_id=to, device_id_type=MESH,
        )
        c.start()
        unsent.append(c)
        return c

    def kspan(k):
        return pl.ds(k * DEPTH, DEPTH)

    load_x = [pltpu.make_async_copy(x_hbm.at[:, kspan(k)], xv.at[:, kspan(k)], load_sem.at[k]) for k in range(4)]
    load_f = [
        [
            pltpu.make_async_copy(
                f_hbm.at[kspan(k), pl.ds(h * COLS, COLS)], fv.at[h, kspan(k), :], load_sem.at[4 + 4 * h + k]
            )
            for k in range(4)
        ]
        for h in range(2)
    ]
    for k in range(4):
        load_x[k].start()
        load_f[0][k].start()
    for k in range(4):
        load_f[1][k].start()
    barrier = pltpu.get_barrier_semaphore()
    everyone = [other, partner] + [yx_peer(j) for j in range(1, 8)] + [z_peer(j) for j in range(1, 8)]
    for to in everyone:
        pl.semaphore_signal(barrier, inc=1, device_id=to, device_id_type=MESH)

    def project(h):
        for k in range(4):
            if h == 0:
                load_x[k].wait()

                def split_x(i, _):
                    r = pl.ds(pl.multiple_of(i * 64, 64), 64)
                    xh[r, kspan(k)], xl[r, kspan(k)] = split(xv[r, kspan(k)])
                    return 0

                lax.fori_loop(0, ROWS // 64, split_x, 0)
            load_f[h][k].wait()

            def split_f(i, _):
                r = pl.ds(pl.multiple_of(k * DEPTH + i * 128, 128), 128)
                fh[h, r, :], fl[h, r, :] = split(fv[h, r, :])
                return 0

            lax.fori_loop(0, DEPTH // 128, split_f, 0)
            part = dot3(xh[:, kspan(k)], xl[:, kspan(k)], fh[h, kspan(k), :], fl[h, kspan(k), :])
            p[h] = part if k == 0 else p[h] + part

    project(0)
    pl.semaphore_wait(barrier, len(everyone))
    proj_copy = [start(p.at[0], pr.at[0], partner)]
    x_copy = start(x_hbm.at[:, pl.ds(pl.multiple_of((1 - core) * MINE, MINE), MINE)], xo, other)
    project(1)
    proj_copy.append(start(p.at[1], pr.at[1], partner))

    def turn(src, base, at):
        def body(i, _):
            c = pl.ds(pl.multiple_of(base + i * 128, 128), 128)
            r = pl.ds(pl.multiple_of(i * 128, 128), 128)
            hi, lo = split(src[:, c].T)
            xth[r, at : at + ROWS] = hi
            xtl[r, at : at + ROWS] = lo
            return 0

        lax.fori_loop(0, MINE // 128, body, 0)

    turn(xv, core * MINE, 0)
    x_copy.wait_recv()
    turn(xo, 0, ROWS)

    def squares(h):
        proj_copy[h].wait_recv()
        total = p[h] + pr[h]
        s[h] = total * total
        return start(s.at[h], so.at[h], other)

    contract = (((0,), (0,)), ((), ()))

    def gram(h):
        cols = slice(h * COLS, (h + 1) * COLS)
        g[:, cols] = jnp.zeros((256, COLS), F32)

        def body(k, _):
            r = pl.ds(pl.multiple_of(k * 512, 512), 512)
            g[:, cols] += dot3(fh[core, r, :], fl[core, r, :], fh[h, r, :], fl[h, r, :], contract)
            return 0

        lax.fori_loop(0, HALF // 512, body, 0)

    def stacked(h):
        ah, al = split(s[h])
        bh, bl = split(so[h])
        return jnp.concatenate([ah, bh], axis=0), jnp.concatenate([al, bl], axis=0)

    def moment(h, sh, sl, at, n):
        r = pl.ds(pl.multiple_of(at, n), n)
        mom[h, r, :] = dot3(xth[r, :], xtl[r, :], sh, sl)

    s_copy = squares(0)
    gram(0)
    s_copy.wait_recv()

    y_copy = {}
    sh, sl = stacked(0)

    def y_send(j, q):
        y_copy[(j, q)] = start(
            mom.at[0, pl.ds(pl.multiple_of(y_of(j) * 256, 256), 256), pl.ds(q * 128, 128)],
            yrecv.at[q, j - 1], y_peer(j),
        )

    for j in (2, 1, 3):
        moment(0, sh, sl, y_of(j) * 256, 256)
        y_send(j, 0)
    for j in (2, 1, 3):
        y_send(j, 1)
    moment(0, sh, sl, y * 256, 256)

    s_copy = squares(1)
    gram(1)
    g_copy = start(g, gr, partner)
    s_copy.wait_recv()
    sh, sl = stacked(1)

    def zrows(zz, half):
        return pl.ds(pl.multiple_of(zz * 128 + half * 64, 64), 64)

    ring_copy = {}

    def ring_hop(i, k):
        way, half, hops = STREAMS[i]
        if k > hops:
            return
        r = zrows(z_of(way * (hops + 1 - k)), half)
        if k > 1:
            ring_copy[(i, k - 1)].wait_recv()
            mom[1, r, :] += ring[SLOT[(i, k - 1)]]
        ring_copy[(i, k)] = start(mom.at[1, r, :], ring.at[SLOT[(i, k)]], z_peer(way))

    def ring_step(k):
        for i in range(4):
            ring_hop(i, k)

    moment(1, sh, sl, z_of(4) * 128, 128)
    ring_hop(0, 1)
    ring_hop(1, 1)
    moment(1, sh, sl, z_of(3) * 128, 128)
    ring_hop(2, 1)
    moment(1, sh, sl, z_of(-3) * 128, 128)
    ring_hop(3, 1)
    for j in (2, -2, 1, -1, 0):
        moment(1, sh, sl, z_of(j) * 128, 128)

    ring_step(2)

    g_copy.wait_recv()
    whole = (g[...] + gr[...]) * (1.0 / D)
    g2[core] = whole * whole
    g2_copy = start(g2.at[core], g2.at[core], other)

    xb_copy = {}
    zb_copy = {}

    def y_sum(q):
        for j in (1, 3, 2):
            y_copy[(j, q)].wait_recv()
        mine = mom[0, pl.ds(pl.multiple_of(y * 256, 256), 256), pl.ds(q * 128, 128)]
        acc_b[q] = (mine + yrecv[q, 0]) + (yrecv[q, 1] + yrecv[q, 2])
        xb_copy[q] = start(acc_b.at[q, pl.ds(pl.multiple_of((1 - xhi) * 128, 128), 128), :], xrecv.at[q], yx_peer(1))

    def x_sum(q):
        xb_copy[q].wait_recv()
        acc_b2[q] = acc_b[q, pl.ds(pl.multiple_of(xhi * 128, 128), 128), :] + xrecv[q]
        for j in (4, 3, 5, 2, 6, 1, 7):
            zb_copy[(j, q)] = start(acc_b2.at[q, span(z_of(j) * 16, 16), :], zrecv.at[q, j - 1], z_peer(j))

    y_sum(0)
    ring_step(3)
    row = (y * 256 + xhi * 128 + z * 16, z * 128 + y * 32 + xhi * 16)
    g2_copy.wait_recv()
    for h in range(2):
        part = jnp.zeros((16, COLS), F32)
        for q in range(2):
            ah, al = split(fv[q, span(core * MINE + row[h], 16), :] * (1.0 / 64.0))
            bh, bl = split(g2[q, :, h * COLS : (h + 1) * COLS])
            part += dot3(ah, al, bh, bl)
        term[h] = part
    x_sum(0)
    y_sum(1)
    ring_step(4)
    x_sum(1)

    for half in range(2):
        parts = []
        for i, (way, h, hops) in enumerate(STREAMS):
            if h == half:
                ring_copy[(i, hops)].wait_recv()
                parts.append(ring[SLOT[(i, hops)]])
        acc_a[half * 64 : half * 64 + 64, :] = mom[1, zrows(z, half), :] + (parts[0] + parts[1])
    da_copy = {}
    for j in (5, 4, 1, 3, 7, 2, 6):
        a, b = yx_of(j)
        da_copy[j] = start(acc_a.at[span(a * 32 + b * 16, 16), :], dir_a.at[j - 1], yx_peer(j))

    def finish(h, total):
        return (6.0 / 64.0) * (term[h] - total * (1.0 / (NROWS * D)))

    base = core * MINE
    forward = []
    waiting = []
    rate = []

    def update(h, at, n):
        r = span(at, n)
        o_ref[r, h * COLS : (h + 1) * COLS] = fv[h, r, :] - grad[h, r, :] * rate[0]

    def arrived(h, at, n):
        r = span(base + at, n)
        c = start(grad.at[h, r, :], grad.at[h, r, :], other)
        forward.append((c, h, at, n))
        if rate:
            update(h, base + at, n)
        else:
            waiting.append((h, at, n))

    owns = []
    for q in range(2):
        part = acc_b2[q, span(z * 16, 16), :]
        for j in range(1, 8):
            zb_copy[(j, q)].wait_recv()
        for j in range(1, 8):
            part = part + zrecv[q, j - 1]
        owns.append(part)
    gb = finish(0, jnp.concatenate(owns, axis=1))
    mine_b = span(base + row[0], 16)
    grad[0, mine_b, :] = gb
    zg_copy = [start(grad.at[0, mine_b, :], grad.at[0, mine_b, :], z_peer(j)) for j in (4, 3, 5, 2, 6, 1, 7)]

    own = acc_a[span(y * 32 + xhi * 16, 16), :]
    for j in range(1, 8):
        da_copy[j].wait_recv()
    for j in range(1, 8):
        own = own + dir_a[j - 1]
    ga = finish(1, own)
    mine_a = span(base + row[1], 16)
    grad[1, mine_a, :] = ga
    aa_copy = [start(grad.at[1, mine_a, :], grad.at[1, mine_a, :], yx_peer(j)) for j in (5, 4, 1, 3, 7, 2, 6)]

    sq = ga * ga + gb * gb
    tile = (sq[0:8, 0:128] + sq[8:16, 0:128]) + (sq[0:8, 128:256] + sq[8:16, 128:256])
    me1 = y * 2 + xhi
    ss1[me1] = tile
    s1_copy = [start(ss1.at[me1], ss1.at[me1], yx_peer(j)) for j in range(1, 8)]

    for c in zg_copy:
        c.wait_recv()
    yg_copy = {}

    def y_spread(i):
        at = y * 256 + (xhi * 128 if i == 0 else (1 - xhi) * 128)
        r = span(base + at, 128)
        for q in (2, 1, 3):
            yg_copy[(i, q)] = start(grad.at[0, r, :], grad.at[0, r, :], y_peer(q))
        arrived(0, at, 128)

    r = span(base + y * 256 + xhi * 128, 128)
    xg_copy = start(grad.at[0, r, :], grad.at[0, r, :], yx_peer(1))
    y_spread(0)

    for c in aa_copy:
        c.wait_recv()
    gather = {}

    def gather_step(k):
        for i, (way, half, hops) in enumerate(STREAMS):
            if k > hops + 1:
                continue
            at = z_of(-way * (k - 1)) * 128 + half * 64
            r = span(base + at, 64)
            if k > 1:
                gather[(i, k - 1)].wait_recv()
            if k <= hops:
                gather[(i, k)] = start(grad.at[1, r, :], grad.at[1, r, :], z_peer(way))
            if k > 1:
                arrived(1, at, 64)

    gather_step(1)
    arrived(1, z * 128, 128)
    for c in s1_copy:
        c.wait_recv()
    tile = ss1[0]
    for j in range(1, 8):
        tile = tile + ss1[j]
    ss2[z] = tile
    s2_copy = [start(ss2.at[z], ss2.at[z], z_peer(j)) for j in range(1, 8)]
    xg_copy.wait_recv()
    y_spread(1)
    gather_step(2)
    for c in s2_copy:
        c.wait_recv()
    tile = ss2[0]
    for j in range(1, 8):
        tile = tile + ss2[j]
    ss3[core] = tile
    s3_copy = start(ss3.at[core], ss3.at[core], other)
    gather_step(3)
    s3_copy.wait_recv()
    ss4[feat] = ss3[0] + ss3[1]
    s4_copy = start(ss4.at[feat], ss4.at[feat], partner)
    gather_step(4)
    s4_copy.wait_recv()
    total = jnp.sum(ss4[0] + ss4[1], keepdims=True)
    rms = jnp.sqrt(total * (1.0 / (D * R))) + 1e-06
    rate.append(0.5 / rms)
    for h, at, n in waiting:
        update(h, base + at, n)
    over = (1 - core) * MINE

    def from_other(upto):
        while len(done) < upto:
            c, h, at, n = forward[len(done)]
            c.wait_recv()
            update(h, over + at, n)
            done.append(0)

    done = []
    from_other(len(forward))

    def y_land(i):
        for q in (1, 3, 2):
            yg_copy[(i, q)].wait_recv()
            arrived(0, y_of(-q) * 256 + (xhi * 128 if i == 0 else (1 - xhi) * 128), 128)

    y_land(0)
    gather_step(5)
    from_other(len(forward) - 4)
    y_land(1)
    from_other(len(forward))
    for c in unsent:
        c.wait_send()


NSEM = 224


def per_device(samples, factor):
    vm = pltpu.VMEM
    scratch = [
        vm((ROWS, HALF), F32), vm((ROWS, MINE), F32), vm((2, HALF, COLS), F32),
        vm((2, HALF, COLS), BF16), vm((2, HALF, COLS), BF16),
        vm((ROWS, HALF), BF16), vm((ROWS, HALF), BF16),
        vm((2, ROWS, COLS), F32), vm((2, ROWS, COLS), F32), vm((2, ROWS, COLS), F32), vm((2, ROWS, COLS), F32),
        vm((MINE, 2 * ROWS), BF16), vm((MINE, 2 * ROWS), BF16), vm((2, MINE, COLS), F32),
        vm((NSLOT, 64, COLS), F32), vm((128, COLS), F32), vm((7, 16, COLS), F32),
        vm((2, 3, 256, 128), F32), vm((2, 256, 128), F32), vm((2, 7, 16, 128), F32),
        vm((2, 128, 128), F32), vm((2, 128, 128), F32),
        vm((256, R), F32), vm((256, R), F32), vm((2, 256, R), F32), vm((2, 16, COLS), F32),
        vm((2, HALF, COLS), F32),
        vm((8, 8, 128), F32), vm((8, 8, 128), F32), vm((2, 8, 128), F32), vm((2, 8, 128), F32),
        pltpu.SemaphoreType.DMA((12,)), pltpu.SemaphoreType.DMA((NSEM,)), pltpu.SemaphoreType.DMA((NSEM,)),
    ]
    return pl.pallas_call(
        kernel,
        out_shape=pltpu.VMEM((HALF, R), F32),
        in_specs=[pl.BlockSpec(memory_space=pltpu.HBM)] * 2,
        out_specs=pl.BlockSpec(memory_space=pltpu.VMEM),
        scratch_shapes=scratch,
        name="cp_step",
        cost_estimate=pl.CostEstimate(flops=10**10, bytes_accessed=10**7, transcendentals=0),
        compiler_params=pltpu.CompilerParams(
            collective_id=0, has_side_effects=True, vmem_limit_bytes=50 * 2**20
        ),
    )(samples, factor)


def solution(mesh):
    placed = (P("samples", "feat"), P("feat", None))
    return jax.shard_map(
        per_device, mesh=mesh, in_specs=placed, out_specs=P("feat", None), check_vma=False
    )
```

```python
import jax
import jax.numpy as jnp
from jax import lax
from jax.experimental import pallas as pl
from jax.experimental.pallas import tpu as pltpu
from jax.sharding import PartitionSpec as P

D = 4096
R = 512
NROWS = 32768
HALF = D // 2
ROWS = 256
COLS = 256
DEPTH = 512
MINE = HALF // 2
MESH = pl.DeviceIdType.MESH
F32 = jnp.float32
BF16 = jnp.bfloat16

STREAMS = ((1, 0, 4), (-1, 1, 4), (1, 1, 3), (-1, 0, 3))
SLOT = {}
for _k in range(1, 5):
    for _i, (_, _, _hops) in enumerate(STREAMS):
        if _k <= _hops:
            SLOT[(_i, _k)] = len(SLOT)
NSLOT = len(SLOT)


def split(v):
    hi = v.astype(BF16)
    return hi, (v - hi.astype(F32)).astype(BF16)


def dot3(ah, al, bh, bl, dims=(((1,), (0,)), ((), ()))):
    def one(a, b):
        return lax.dot_general(a, b, dims, preferred_element_type=F32)

    return one(ah, bh) + (one(ah, bl) + one(al, bh))


def kernel(
    x_hbm, f_hbm, o_ref,
    xv, xo, fv, fh, fl, xh, xl, p, pr, s, so, xth, xtl, mom,
    ring, acc_a, dir_a, yrecv, acc_b, zrecv, acc_b2, xrecv,
    gram, gram_mine, gram_other, wh, wl, grad, ss1, ss2, ss3, ss4,
    load_sem, send, recv,
):
    sidx = lax.axis_index("samples")
    feat = lax.axis_index("feat")
    core = lax.rem(sidx, 2)
    z = lax.rem(sidx // 2, 8)
    y = lax.rem(sidx // 16, 4)
    xhi = sidx // 64

    def dev(a, b, c, d, e):
        return (((a * 4 + b) * 8 + c) * 2 + d, e)

    other = dev(xhi, y, z, 1 - core, feat)
    partner = dev(xhi, y, z, core, 1 - feat)

    def yx_of(j):
        return lax.rem(y + j // 2, 4), lax.rem(xhi + j % 2, 2)

    def yx_peer(j):
        a, b = yx_of(j)
        return dev(b, a, z, core, feat)

    def y_of(j):
        return lax.rem(y + j + 4, 4)

    def y_peer(j):
        return dev(xhi, y_of(j), z, core, feat)

    def z_of(j):
        return lax.rem(z + j + 8, 8)

    def z_peer(j):
        return dev(xhi, y, z_of(j), core, feat)

    def span(at, n):
        return pl.ds(pl.multiple_of(at, 16), n)

    counter = [0]
    unsent = []

    def start(src, dst, to):
        i = counter[0]
        counter[0] += 1
        c = pltpu.make_async_remote_copy(
            src_ref=src, dst_ref=dst, send_sem=send.at[i], recv_sem=recv.at[i],
            device_id=to, device_id_type=MESH,
        )
        c.start()
        unsent.append(c)
        return c

    def kspan(k):
        return pl.ds(k * DEPTH, DEPTH)

    load_x = [pltpu.make_async_copy(x_hbm.at[:, kspan(k)], xv.at[:, kspan(k)], load_sem.at[k]) for k in range(4)]
    load_f = [
        [
            pltpu.make_async_copy(
                f_hbm.at[kspan(k), pl.ds(h * COLS, COLS)], fv.at[h, kspan(k), :], load_sem.at[4 + 4 * h + k]
            )
            for k in range(4)
        ]
        for h in range(2)
    ]
    for k in range(4):
        load_x[k].start()
        load_f[0][k].start()
    for k in range(4):
        load_f[1][k].start()
    barrier = pltpu.get_barrier_semaphore()
    everyone = [other, partner] + [yx_peer(j) for j in range(1, 8)] + [z_peer(j) for j in range(1, 8)]
    for to in everyone:
        pl.semaphore_signal(barrier, inc=1, device_id=to, device_id_type=MESH)

    def split_factor(h, k):
        load_f[h][k].wait()

        def body(i, _):
            r = pl.ds(pl.multiple_of(k * DEPTH + i * 128, 128), 128)
            fh[h, r, :], fl[h, r, :] = split(fv[h, r, :])
            return 0

        lax.fori_loop(0, DEPTH // 128, body, 0)

    def project(h):
        for k in range(4):
            if h == 0:
                load_x[k].wait()

                def split_x(i, _):
                    r = pl.ds(pl.multiple_of(i * 64, 64), 64)
                    xh[r, kspan(k)], xl[r, kspan(k)] = split(xv[r, kspan(k)])
                    return 0

                lax.fori_loop(0, ROWS // 64, split_x, 0)
            if h == 0:
                split_factor(0, k)
            part = dot3(xh[:, kspan(k)], xl[:, kspan(k)], fh[h, kspan(k), :], fl[h, kspan(k), :])
            for i in range(2):
                piece = part[:, i * 128 : (i + 1) * 128]
                p[2 * h + i] = piece if k == 0 else p[2 * h + i] + piece

    proj_copy = {}

    def exchange(h):
        for q in (2 * h, 2 * h + 1):
            proj_copy[q] = start(p.at[q], pr.at[q], partner)

    project(0)
    pl.semaphore_wait(barrier, len(everyone))
    exchange(0)
    x_copy = start(x_hbm.at[:, pl.ds(pl.multiple_of((1 - core) * MINE, MINE), MINE)], xo, other)
    for k in range(4):
        split_factor(1, k)

    contract = (((0,), (0,)), ((), ()))
    chip = (xhi * 4 + y) * 8 + z
    block = chip // 16
    block_at = pl.ds(pl.multiple_of(lax.rem(block, 2) * 128, 128), 128)
    block_half = block // 2
    eight = pl.ds(pl.multiple_of(lax.rem(chip, 16) * 8, 8), 8)
    for h in range(2):
        cols = slice(h * COLS, (h + 1) * COLS)
        for k in range(4):
            part = dot3(
                fh[block_half, kspan(k), block_at], fl[block_half, kspan(k), block_at],
                fh[h, kspan(k), :], fl[h, kspan(k), :], contract,
            )
            gram[:, cols] = part if k == 0 else gram[:, cols] + part
    gram_mine[...] = gram[eight, :]
    g_copy = start(gram_mine, gram_other, partner)

    project(1)
    exchange(1)

    def turn(src, base, at):
        def body(i, _):
            c = pl.ds(pl.multiple_of(base + i * 128, 128), 128)
            r = pl.ds(pl.multiple_of(i * 128, 128), 128)
            hi, lo = split(src[:, c].T)
            xth[r, at : at + ROWS] = hi
            xtl[r, at : at + ROWS] = lo
            return 0

        lax.fori_loop(0, MINE // 128, body, 0)

    turn(xv, core * MINE, 0)
    x_copy.wait_recv()
    turn(xo, 0, ROWS)

    base = core * MINE
    s_copy = {}

    def squares(q):
        proj_copy[q].wait_recv()
        total = p[q] + pr[q]
        s[q] = total * total
        s_copy[q] = start(s.at[q], so.at[q], other)

    def stacked(q):
        s_copy[q].wait_recv()
        ah, al = split(s[q])
        bh, bl = split(so[q])
        return jnp.concatenate([ah, bh], axis=0), jnp.concatenate([al, bl], axis=0)

    def moment(q, sh, sl, at, n):
        r = pl.ds(pl.multiple_of(at, n), n)
        w = pl.ds(pl.multiple_of(base + at, n), n)
        cols = slice(q * 128, (q + 1) * 128)
        mom[q, r, :] = dot3(xth[r, :], xtl[r, :], sh, sl) - dot3(
            fh[block_half, w, block_at], fl[block_half, w, block_at], wh[:, cols], wl[:, cols]
        )

    y_copy, xb_copy, zb_copy = {}, {}, {}

    def y_start(q):
        sh, sl = stacked(q)
        for j in (2, 1, 3):
            moment(q, sh, sl, y_of(j) * 256, 256)
            y_copy[(j, q)] = start(
                mom.at[q, pl.ds(pl.multiple_of(y_of(j) * 256, 256), 256), :], yrecv.at[q // 2, j - 1], y_peer(j)
            )
        moment(q, sh, sl, y * 256, 256)

    def y_sum(q):
        for j in (1, 3, 2):
            y_copy[(j, q)].wait_recv()
        i = q // 2
        mine = mom[q, pl.ds(pl.multiple_of(y * 256, 256), 256), :]
        acc_b[i] = (mine + yrecv[i, 0]) + (yrecv[i, 1] + yrecv[i, 2])
        xb_copy[q] = start(acc_b.at[i, pl.ds(pl.multiple_of((1 - xhi) * 128, 128), 128), :], xrecv.at[i], yx_peer(1))

    def x_sum(q):
        i = q // 2
        xb_copy[q].wait_recv()
        acc_b2[i] = acc_b[i, pl.ds(pl.multiple_of(xhi * 128, 128), 128), :] + xrecv[i]
        for j in (4, 3, 5, 2, 6, 1, 7):
            zb_copy[(j, q)] = start(acc_b2.at[i, span(z_of(j) * 16, 16), :], zrecv.at[i, j - 1], z_peer(j))

    def z_sum(q):
        i = q // 2
        part = acc_b2[i, span(z * 16, 16), :]
        for j in range(1, 8):
            zb_copy[(j, q)].wait_recv()
        for j in range(1, 8):
            part = part + zrecv[i, j - 1]
        return part

    def zrows(zz, half):
        return pl.ds(pl.multiple_of(zz * 128 + half * 64, 64), 64)

    ring_copy, da_copy = {}, {}

    def ring_hop(q, i, k):
        way, half, hops = STREAMS[i]
        if k > hops:
            return
        r = zrows(z_of(way * (hops + 1 - k)), half)
        if k > 1:
            ring_copy[(q, i, k - 1)].wait_recv()
            mom[q, r, :] += ring[q // 2, SLOT[(i, k - 1)]]
        ring_copy[(q, i, k)] = start(mom.at[q, r, :], ring.at[q // 2, SLOT[(i, k)]], z_peer(way))

    def ring_step(q, k):
        for i in range(4):
            ring_hop(q, i, k)

    def ring_start(q):
        sh, sl = stacked(q)
        moment(q, sh, sl, z_of(4) * 128, 128)
        ring_hop(q, 0, 1)
        ring_hop(q, 1, 1)
        moment(q, sh, sl, z_of(3) * 128, 128)
        ring_hop(q, 2, 1)
        moment(q, sh, sl, z_of(-3) * 128, 128)
        ring_hop(q, 3, 1)
        for j in (2, -2, 1, -1, 0):
            moment(q, sh, sl, z_of(j) * 128, 128)

    def ring_end(q):
        for half in range(2):
            parts = []
            for i, (way, h, hops) in enumerate(STREAMS):
                if h == half:
                    ring_copy[(q, i, hops)].wait_recv()
                    parts.append(ring[q // 2, SLOT[(i, hops)]])
            acc_a[q // 2, half * 64 : half * 64 + 64, :] = mom[q, zrows(z, half), :] + (parts[0] + parts[1])
        for j in (5, 4, 1, 3, 7, 2, 6):
            a, b = yx_of(j)
            da_copy[(j, q)] = start(acc_a.at[q // 2, span(a * 32 + b * 16, 16), :], dir_a.at[q // 2, j - 1], yx_peer(j))

    def direct_sum(q):
        part = acc_a[q // 2, span(y * 32 + xhi * 16, 16), :]
        for j in range(1, 8):
            da_copy[(j, q)].wait_recv()
        for j in range(1, 8):
            part = part + dir_a[q // 2, j - 1]
        return part

    def gram_weights():
        gram[...] = jnp.zeros_like(gram)
        g_copy.wait_recv()
        whole = (gram_mine[...] + gram_other[...]) * (1.0 / D)
        gram[eight, :] = whole * whole * (NROWS * D / 64.0)
        wh[...], wl[...] = split(gram[...])

    row = (y * 256 + xhi * 128 + z * 16, z * 128 + y * 32 + xhi * 16)

    squares_of = []

    def finish(q, total):
        gq = total * (-6.0 / 64.0 / (NROWS * D))
        squares_of.append(gq * gq)
        grad[q, span(base + row[q % 2], 16), :] = gq

    forward = []
    waiting = []
    rate = []
    zg_copy, xg_copy, yg_copy, aa_copy, gather = {}, {}, {}, {}, {}

    def update(q, at, n):
        r = span(at, n)
        c = (q % 2) * 128
        o_ref[r, q * 128 : (q + 1) * 128] = fv[q // 2, r, c : c + 128] - grad[q, r, :] * rate[0]

    def send_rows(q, at, n, to):
        r = span(base + at, n)
        return start(grad.at[q, r, :], grad.at[q, r, :], to)

    def arrived(q, at, n):
        forward.append((send_rows(q, at, n, other), q, at, n))
        if rate:
            update(q, base + at, n)
        else:
            waiting.append((q, at, n))

    def own_y(q):
        finish(q, z_sum(q))
        zg_copy[q] = [send_rows(q, row[0], 16, z_peer(j)) for j in (4, 3, 5, 2, 6, 1, 7)]

    def own_ring(q):
        finish(q, direct_sum(q))
        aa_copy[q] = [send_rows(q, row[1], 16, yx_peer(j)) for j in (5, 4, 1, 3, 7, 2, 6)]

    def y_rows(yy, i):
        return yy * 256 + (xhi * 128 if i == 0 else (1 - xhi) * 128)

    def y_spread(q, i):
        at = y_rows(y, i)
        if i == 0:
            for c in zg_copy[q]:
                c.wait_recv()
            xg_copy[q] = send_rows(q, at, 128, yx_peer(1))
        else:
            xg_copy[q].wait_recv()
        for j in (2, 1, 3):
            yg_copy[(q, i, j)] = send_rows(q, at, 128, y_peer(j))
        arrived(q, at, 128)

    def y_land(q, i):
        for j in (1, 3, 2):
            yg_copy[(q, i, j)].wait_recv()
            arrived(q, y_rows(y_of(-j), i), 128)

    def gather_step(q, k):
        if k == 1:
            for c in aa_copy[q]:
                c.wait_recv()
        for i, (way, half, hops) in enumerate(STREAMS):
            if k > hops + 1:
                continue
            at = z_of(-way * (k - 1)) * 128 + half * 64
            if k > 1:
                gather[(q, i, k - 1)].wait_recv()
            if k <= hops:
                gather[(q, i, k)] = send_rows(q, at, 64, z_peer(way))
            if k > 1:
                arrived(q, at, 64)
        if k == 1:
            arrived(q, z * 128, 128)

    done = []

    def from_other(upto):
        while len(done) < upto:
            c, q, at, n = forward[len(done)]
            c.wait_recv()
            update(q, (1 - core) * MINE + at, n)
            done.append(0)

    squares(0)
    gram_weights()
    y_start(0)
    squares(1)
    ring_start(1)
    squares(2)
    y_start(2)
    squares(3)
    ring_step(1, 2)
    ring_start(3)
    ring_step(1, 3)
    y_sum(0)
    ring_step(3, 2)
    ring_step(1, 4)
    x_sum(0)
    ring_step(3, 3)
    y_sum(2)
    ring_end(1)
    own_y(0)
    ring_step(3, 4)
    x_sum(2)
    own_ring(1)
    ring_end(3)
    y_spread(0, 0)
    own_y(2)
    gather_step(1, 1)
    own_ring(3)
    sq = (squares_of[0] + squares_of[1]) + (squares_of[2] + squares_of[3])
    me1 = y * 2 + xhi
    ss1[me1] = sq[0:8] + sq[8:16]
    s1_copy = [start(ss1.at[me1], ss1.at[me1], yx_peer(j)) for j in range(1, 8)]
    y_spread(0, 1)
    y_spread(2, 0)
    gather_step(1, 2)
    for c in s1_copy:
        c.wait_recv()
    tile = ss1[0]
    for j in range(1, 8):
        tile = tile + ss1[j]
    ss2[z] = tile
    s2_copy = [start(ss2.at[z], ss2.at[z], z_peer(j)) for j in range(1, 8)]
    gather_step(3, 1)
    gather_step(1, 3)
    y_spread(2, 1)
    gather_step(3, 2)
    gather_step(1, 4)
    for c in s2_copy:
        c.wait_recv()
    tile = ss2[0]
    for j in range(1, 8):
        tile = tile + ss2[j]
    ss3[core] = tile
    s3_copy = start(ss3.at[core], ss3.at[core], other)
    y_land(0, 0)
    s3_copy.wait_recv()
    ss4[feat] = ss3[0] + ss3[1]
    s4_copy = start(ss4.at[feat], ss4.at[feat], partner)
    y_land(0, 1)
    gather_step(3, 3)
    gather_step(1, 5)
    s4_copy.wait_recv()
    total = jnp.sum(ss4[0] + ss4[1], keepdims=True)
    rms = jnp.sqrt(total * (1.0 / (D * R))) + 1e-06
    rate.append(0.5 / rms)
    for q, at, n in waiting:
        update(q, base + at, n)
    gather_step(3, 4)
    y_land(2, 0)
    from_other(len(forward) - 8)
    y_land(2, 1)
    gather_step(3, 5)
    from_other(len(forward))
    for c in unsent:
        c.wait_send()


NSEM = 256


def per_device(samples, factor):
    vm = pltpu.VMEM
    scratch = [
        vm((ROWS, HALF), F32), vm((ROWS, MINE), F32), vm((2, HALF, COLS), F32),
        vm((2, HALF, COLS), BF16), vm((2, HALF, COLS), BF16),
        vm((ROWS, HALF), BF16), vm((ROWS, HALF), BF16),
        vm((4, ROWS, 128), F32), vm((4, ROWS, 128), F32), vm((4, ROWS, 128), F32), vm((4, ROWS, 128), F32),
        vm((MINE, 2 * ROWS), BF16), vm((MINE, 2 * ROWS), BF16), vm((4, MINE, 128), F32),
        vm((2, NSLOT, 64, 128), F32), vm((2, 128, 128), F32), vm((2, 7, 16, 128), F32),
        vm((2, 3, 256, 128), F32), vm((2, 256, 128), F32), vm((2, 7, 16, 128), F32),
        vm((2, 128, 128), F32), vm((2, 128, 128), F32),
        vm((128, R), F32), vm((8, R), F32), vm((8, R), F32), vm((128, R), BF16), vm((128, R), BF16),
        vm((4, HALF, 128), F32),
        vm((8, 8, 128), F32), vm((8, 8, 128), F32), vm((2, 8, 128), F32), vm((2, 8, 128), F32),
        pltpu.SemaphoreType.DMA((12,)), pltpu.SemaphoreType.DMA((NSEM,)), pltpu.SemaphoreType.DMA((NSEM,)),
    ]
    return pl.pallas_call(
        kernel,
        out_shape=pltpu.VMEM((HALF, R), F32),
        in_specs=[pl.BlockSpec(memory_space=pltpu.HBM)] * 2,
        out_specs=pl.BlockSpec(memory_space=pltpu.VMEM),
        scratch_shapes=scratch,
        name="cp_step",
        cost_estimate=pl.CostEstimate(flops=10**10, bytes_accessed=10**7, transcendentals=0),
        compiler_params=pltpu.CompilerParams(
            collective_id=0, has_side_effects=True, vmem_limit_bytes=50 * 2**20
        ),
    )(samples, factor)


def solution(mesh):
    placed = (P("samples", "feat"), P("feat", None))
    return jax.shard_map(
        per_device, mesh=mesh, in_specs=placed, out_specs=P("feat", None), check_vma=False
    )
```

```python
import jax
import jax.numpy as jnp
from jax import lax
from jax.experimental import pallas as pl
from jax.experimental.pallas import tpu as pltpu
from jax.sharding import PartitionSpec as P

D = 4096
R = 512
NROWS = 32768
HALF = D // 2
ROWS = 256
COLS = 256
DEPTH = 512
MINE = HALF // 2
MESH = pl.DeviceIdType.MESH
F32 = jnp.float32
BF16 = jnp.bfloat16

STREAMS = ((1, 0, 4), (-1, 1, 4), (1, 1, 3), (-1, 0, 3))
SLOT = {}
for _k in range(1, 5):
    for _i, (_, _, _hops) in enumerate(STREAMS):
        if _k <= _hops:
            SLOT[(_i, _k)] = len(SLOT)
NSLOT = len(SLOT)


def split(v):
    hi = v.astype(BF16)
    return hi, (v - hi.astype(F32)).astype(BF16)


def dot3(ah, al, bh, bl, dims=(((1,), (0,)), ((), ()))):
    def one(a, b):
        return lax.dot_general(a, b, dims, preferred_element_type=F32)

    return one(ah, bh) + (one(ah, bl) + one(al, bh))


def kernel(
    x_hbm, f_hbm, o_ref,
    xv, xo, fv, fh, fl, xh, xl, p, pr, s, so, xth, xtl, mom,
    ring, acc_a, dir_a, yrecv, acc_b, zrecv, acc_b2, xrecv,
    gram, gram_mine, gram_other, wh, wl, grad, ss1, ss2, ss3, ss4,
    load_sem, send, recv,
):
    sidx = lax.axis_index("samples")
    feat = lax.axis_index("feat")
    core = lax.rem(sidx, 2)
    z = lax.rem(sidx // 2, 8)
    y = lax.rem(sidx // 16, 4)
    xhi = sidx // 64

    def dev(a, b, c, d, e):
        return (((a * 4 + b) * 8 + c) * 2 + d, e)

    other = dev(xhi, y, z, 1 - core, feat)
    partner = dev(xhi, y, z, core, 1 - feat)

    def yx_of(j):
        return lax.rem(y + j // 2, 4), lax.rem(xhi + j % 2, 2)

    def yx_peer(j):
        a, b = yx_of(j)
        return dev(b, a, z, core, feat)

    def y_of(j):
        return lax.rem(y + j + 4, 4)

    def y_peer(j):
        return dev(xhi, y_of(j), z, core, feat)

    def z_of(j):
        return lax.rem(z + j + 8, 8)

    def z_peer(j):
        return dev(xhi, y, z_of(j), core, feat)

    def span(at, n):
        return pl.ds(pl.multiple_of(at, 16), n)

    counter = [0]
    unsent = []

    def start(src, dst, to):
        i = counter[0]
        counter[0] += 1
        c = pltpu.make_async_remote_copy(
            src_ref=src, dst_ref=dst, send_sem=send.at[i], recv_sem=recv.at[i],
            device_id=to, device_id_type=MESH,
        )
        c.start()
        unsent.append(c)
        return c

    def kspan(k):
        return pl.ds(k * DEPTH, DEPTH)

    load_x = [pltpu.make_async_copy(x_hbm.at[:, kspan(k)], xv.at[:, kspan(k)], load_sem.at[k]) for k in range(4)]
    load_f = [
        [
            pltpu.make_async_copy(
                f_hbm.at[kspan(k), pl.ds(h * COLS, COLS)], fv.at[h, kspan(k), :], load_sem.at[4 + 4 * h + k]
            )
            for k in range(4)
        ]
        for h in range(2)
    ]
    for k in range(4):
        load_x[k].start()
        load_f[0][k].start()
    for k in range(4):
        load_f[1][k].start()
    barrier = pltpu.get_barrier_semaphore()
    everyone = [other, partner] + [yx_peer(j) for j in range(1, 8)] + [z_peer(j) for j in range(1, 8)]
    for to in everyone:
        pl.semaphore_signal(barrier, inc=1, device_id=to, device_id_type=MESH)

    def split_factor(h, k):
        load_f[h][k].wait()

        def body(i, _):
            r = pl.ds(pl.multiple_of(k * DEPTH + i * 128, 128), 128)
            fh[h, r, :], fl[h, r, :] = split(fv[h, r, :])
            return 0

        lax.fori_loop(0, DEPTH // 128, body, 0)

    def project(h):
        for k in range(4):
            if h == 0:
                load_x[k].wait()

                def split_x(i, _):
                    r = pl.ds(pl.multiple_of(i * 64, 64), 64)
                    xh[r, kspan(k)], xl[r, kspan(k)] = split(xv[r, kspan(k)])
                    return 0

                lax.fori_loop(0, ROWS // 64, split_x, 0)
            if h == 0:
                split_factor(0, k)
            part = dot3(xh[:, kspan(k)], xl[:, kspan(k)], fh[h, kspan(k), :], fl[h, kspan(k), :])
            for i in range(2):
                piece = part[:, i * 128 : (i + 1) * 128]
                p[2 * h + i] = piece if k == 0 else p[2 * h + i] + piece

    proj_copy = {}

    def exchange(h):
        for q in (2 * h, 2 * h + 1):
            proj_copy[q] = start(p.at[q], pr.at[q], partner)

    project(0)
    pl.semaphore_wait(barrier, len(everyone))
    exchange(0)
    x_copy = start(x_hbm.at[:, pl.ds(pl.multiple_of((1 - core) * MINE, MINE), MINE)], xo, other)
    for k in range(4):
        split_factor(1, k)

    contract = (((0,), (0,)), ((), ()))
    chip = (xhi * 4 + y) * 8 + z
    block = chip // 16
    block_at = pl.ds(pl.multiple_of(lax.rem(block, 2) * 128, 128), 128)
    block_half = block // 2
    eight = pl.ds(pl.multiple_of(lax.rem(chip, 16) * 8, 8), 8)
    for h in range(2):
        cols = slice(h * COLS, (h + 1) * COLS)
        for k in range(4):
            part = dot3(
                fh[block_half, kspan(k), block_at], fl[block_half, kspan(k), block_at],
                fh[h, kspan(k), :], fl[h, kspan(k), :], contract,
            )
            gram[:, cols] = part if k == 0 else gram[:, cols] + part
    gram_mine[...] = gram[eight, :]
    g_copy = start(gram_mine, gram_other, partner)

    project(1)
    exchange(1)

    def turn(src, base, at):
        def body(i, _):
            c = pl.ds(pl.multiple_of(base + i * 128, 128), 128)
            r = pl.ds(pl.multiple_of(i * 128, 128), 128)
            hi, lo = split(src[:, c].T)
            xth[r, at : at + ROWS] = hi
            xtl[r, at : at + ROWS] = lo
            return 0

        lax.fori_loop(0, MINE // 128, body, 0)

    turn(xv, core * MINE, 0)
    x_copy.wait_recv()
    turn(xo, 0, ROWS)

    base = core * MINE
    s_copy = {}

    def squares(q):
        proj_copy[q].wait_recv()
        total = p[q] + pr[q]
        s[q] = total * total
        s_copy[q] = start(s.at[q], so.at[q], other)

    def stacked(q):
        s_copy[q].wait_recv()
        ah, al = split(s[q])
        bh, bl = split(so[q])
        return jnp.concatenate([ah, bh], axis=0), jnp.concatenate([al, bl], axis=0)

    def moment(q, sh, sl, at, n):
        r = pl.ds(pl.multiple_of(at, n), n)
        w = pl.ds(pl.multiple_of(base + at, n), n)
        cols = slice(q * 128, (q + 1) * 128)
        mom[q, r, :] = dot3(xth[r, :], xtl[r, :], sh, sl) - dot3(
            fh[block_half, w, block_at], fl[block_half, w, block_at], wh[:, cols], wl[:, cols]
        )

    y_copy, xb_copy, zb_copy = {}, {}, {}

    def y_start(q):
        sh, sl = stacked(q)
        for j in (2, 1, 3):
            moment(q, sh, sl, y_of(j) * 256, 256)
            y_copy[(j, q)] = start(
                mom.at[q, pl.ds(pl.multiple_of(y_of(j) * 256, 256), 256), :], yrecv.at[q // 2, j - 1], y_peer(j)
            )
        moment(q, sh, sl, y * 256, 256)

    def y_sum(q):
        for j in (1, 3, 2):
            y_copy[(j, q)].wait_recv()
        i = q // 2
        mine = mom[q, pl.ds(pl.multiple_of(y * 256, 256), 256), :]
        acc_b[i] = (mine + yrecv[i, 0]) + (yrecv[i, 1] + yrecv[i, 2])
        xb_copy[q] = start(acc_b.at[i, pl.ds(pl.multiple_of((1 - xhi) * 128, 128), 128), :], xrecv.at[i], yx_peer(1))

    def x_sum(q):
        i = q // 2
        xb_copy[q].wait_recv()
        acc_b2[i] = acc_b[i, pl.ds(pl.multiple_of(xhi * 128, 128), 128), :] + xrecv[i]
        for j in (4, 3, 5, 2, 6, 1, 7):
            zb_copy[(j, q)] = start(acc_b2.at[i, span(z_of(j) * 16, 16), :], zrecv.at[i, j - 1], z_peer(j))

    def z_sum(q):
        i = q // 2
        part = acc_b2[i, span(z * 16, 16), :]
        for j in range(1, 8):
            zb_copy[(j, q)].wait_recv()
        for j in range(1, 8):
            part = part + zrecv[i, j - 1]
        return part

    def zrows(zz, half):
        return pl.ds(pl.multiple_of(zz * 128 + half * 64, 64), 64)

    ring_copy, da_copy = {}, {}

    def ring_hop(q, i, k):
        way, half, hops = STREAMS[i]
        if k > hops:
            return
        r = zrows(z_of(way * (hops + 1 - k)), half)
        if k > 1:
            ring_copy[(q, i, k - 1)].wait_recv()
            mom[q, r, :] += ring[q // 2, SLOT[(i, k - 1)]]
        ring_copy[(q, i, k)] = start(mom.at[q, r, :], ring.at[q // 2, SLOT[(i, k)]], z_peer(way))

    def ring_step(q, k):
        for i in range(4):
            ring_hop(q, i, k)

    def ring_start(q):
        sh, sl = stacked(q)
        moment(q, sh, sl, z_of(4) * 128, 128)
        ring_hop(q, 0, 1)
        ring_hop(q, 1, 1)
        moment(q, sh, sl, z_of(3) * 128, 128)
        ring_hop(q, 2, 1)
        moment(q, sh, sl, z_of(-3) * 128, 128)
        ring_hop(q, 3, 1)
        for j in (2, -2, 1, -1, 0):
            moment(q, sh, sl, z_of(j) * 128, 128)

    def ring_end(q):
        for half in range(2):
            parts = []
            for i, (way, h, hops) in enumerate(STREAMS):
                if h == half:
                    ring_copy[(q, i, hops)].wait_recv()
                    parts.append(ring[q // 2, SLOT[(i, hops)]])
            acc_a[q // 2, half * 64 : half * 64 + 64, :] = mom[q, zrows(z, half), :] + (parts[0] + parts[1])
        for j in (5, 4, 1, 3, 7, 2, 6):
            a, b = yx_of(j)
            da_copy[(j, q)] = start(acc_a.at[q // 2, span(a * 32 + b * 16, 16), :], dir_a.at[q // 2, j - 1], yx_peer(j))

    def direct_sum(q):
        part = acc_a[q // 2, span(y * 32 + xhi * 16, 16), :]
        for j in range(1, 8):
            da_copy[(j, q)].wait_recv()
        for j in range(1, 8):
            part = part + dir_a[q // 2, j - 1]
        return part

    def gram_weights():
        gram[...] = jnp.zeros_like(gram)
        g_copy.wait_recv()
        whole = (gram_mine[...] + gram_other[...]) * (1.0 / D)
        gram[eight, :] = whole * whole * (NROWS * D / 64.0)
        wh[...], wl[...] = split(gram[...])

    row = (y * 256 + xhi * 128 + z * 16, z * 128 + y * 32 + xhi * 16)

    squares_of = []

    def finish(q, total):
        gq = total * (-6.0 / 64.0 / (NROWS * D))
        squares_of.append(gq * gq)
        grad[q, span(base + row[1 - q % 2], 16), :] = gq

    forward = []
    waiting = []
    rate = []
    zg_copy, xg_copy, yg_copy, aa_copy, gather = {}, {}, {}, {}, {}

    def update(q, at, n):
        r = span(at, n)
        c = (q % 2) * 128
        o_ref[r, q * 128 : (q + 1) * 128] = fv[q // 2, r, c : c + 128] - grad[q, r, :] * rate[0]

    def send_rows(q, at, n, to):
        r = span(base + at, n)
        return start(grad.at[q, r, :], grad.at[q, r, :], to)

    def arrived(q, at, n):
        forward.append((send_rows(q, at, n, other), q, at, n))
        if rate:
            update(q, base + at, n)
        else:
            waiting.append((q, at, n))

    def own_y(q):
        finish(q, z_sum(q))
        zg_copy[q] = [send_rows(q, row[0], 16, z_peer(j)) for j in (4, 3, 5, 2, 6, 1, 7)]

    def own_ring(q):
        finish(q, direct_sum(q))
        aa_copy[q] = [send_rows(q, row[1], 16, yx_peer(j)) for j in (5, 4, 1, 3, 7, 2, 6)]

    def y_rows(yy, i):
        return yy * 256 + (xhi * 128 if i == 0 else (1 - xhi) * 128)

    def y_spread(q, i):
        at = y_rows(y, i)
        if i == 0:
            for c in zg_copy[q]:
                c.wait_recv()
            xg_copy[q] = send_rows(q, at, 128, yx_peer(1))
        else:
            xg_copy[q].wait_recv()
        for j in (2, 1, 3):
            yg_copy[(q, i, j)] = send_rows(q, at, 128, y_peer(j))
        arrived(q, at, 128)

    def y_land(q, i):
        for j in (1, 3, 2):
            yg_copy[(q, i, j)].wait_recv()
            arrived(q, y_rows(y_of(-j), i), 128)

    def gather_step(q, k):
        if k == 1:
            for c in aa_copy[q]:
                c.wait_recv()
        for i, (way, half, hops) in enumerate(STREAMS):
            if k > hops + 1:
                continue
            at = z_of(-way * (k - 1)) * 128 + half * 64
            if k > 1:
                gather[(q, i, k - 1)].wait_recv()
            if k <= hops:
                gather[(q, i, k)] = send_rows(q, at, 64, z_peer(way))
            if k > 1:
                arrived(q, at, 64)
        if k == 1:
            arrived(q, z * 128, 128)

    done = []

    def from_other(upto):
        while len(done) < upto:
            c, q, at, n = forward[len(done)]
            c.wait_recv()
            update(q, (1 - core) * MINE + at, n)
            done.append(0)

    squares(0)
    gram_weights()
    ring_start(0)
    squares(1)
    y_start(1)
    squares(2)
    ring_step(0, 2)
    ring_start(2)
    squares(3)
    ring_step(0, 3)
    y_start(3)
    ring_step(2, 2)
    ring_step(0, 4)
    y_sum(1)
    ring_step(2, 3)
    ring_end(0)
    x_sum(1)
    ring_step(2, 4)
    y_sum(3)
    own_ring(0)
    own_y(1)
    ring_end(2)
    x_sum(3)
    gather_step(0, 1)
    y_spread(1, 0)
    own_ring(2)
    own_y(3)
    sq = (squares_of[0] + squares_of[1]) + (squares_of[2] + squares_of[3])
    me1 = y * 2 + xhi
    ss1[me1] = sq[0:8] + sq[8:16]
    s1_copy = [start(ss1.at[me1], ss1.at[me1], yx_peer(j)) for j in range(1, 8)]
    y_spread(1, 1)
    gather_step(0, 2)
    for c in s1_copy:
        c.wait_recv()
    tile = ss1[0]
    for j in range(1, 8):
        tile = tile + ss1[j]
    ss2[z] = tile
    s2_copy = [start(ss2.at[z], ss2.at[z], z_peer(j)) for j in range(1, 8)]
    gather_step(2, 1)
    y_spread(3, 0)
    gather_step(0, 3)
    y_spread(3, 1)
    gather_step(2, 2)
    gather_step(0, 4)
    for c in s2_copy:
        c.wait_recv()
    tile = ss2[0]
    for j in range(1, 8):
        tile = tile + ss2[j]
    ss3[core] = tile
    s3_copy = start(ss3.at[core], ss3.at[core], other)
    y_land(1, 0)
    s3_copy.wait_recv()
    ss4[feat] = ss3[0] + ss3[1]
    s4_copy = start(ss4.at[feat], ss4.at[feat], partner)
    y_land(1, 1)
    gather_step(2, 3)
    gather_step(0, 5)
    s4_copy.wait_recv()
    total = jnp.sum(ss4[0] + ss4[1], keepdims=True)
    rms = jnp.sqrt(total * (1.0 / (D * R))) + 1e-06
    rate.append(0.5 / rms)
    for q, at, n in waiting:
        update(q, base + at, n)
    y_land(3, 0)
    gather_step(2, 4)
    from_other(len(forward) - 8)
    y_land(3, 1)
    gather_step(2, 5)
    from_other(len(forward))
    for c in unsent:
        c.wait_send()


NSEM = 256


def per_device(samples, factor):
    vm = pltpu.VMEM
    scratch = [
        vm((ROWS, HALF), F32), vm((ROWS, MINE), F32), vm((2, HALF, COLS), F32),
        vm((2, HALF, COLS), BF16), vm((2, HALF, COLS), BF16),
        vm((ROWS, HALF), BF16), vm((ROWS, HALF), BF16),
        vm((4, ROWS, 128), F32), vm((4, ROWS, 128), F32), vm((4, ROWS, 128), F32), vm((4, ROWS, 128), F32),
        vm((MINE, 2 * ROWS), BF16), vm((MINE, 2 * ROWS), BF16), vm((4, MINE, 128), F32),
        vm((2, NSLOT, 64, 128), F32), vm((2, 128, 128), F32), vm((2, 7, 16, 128), F32),
        vm((2, 3, 256, 128), F32), vm((2, 256, 128), F32), vm((2, 7, 16, 128), F32),
        vm((2, 128, 128), F32), vm((2, 128, 128), F32),
        vm((128, R), F32), vm((8, R), F32), vm((8, R), F32), vm((128, R), BF16), vm((128, R), BF16),
        vm((4, HALF, 128), F32),
        vm((8, 8, 128), F32), vm((8, 8, 128), F32), vm((2, 8, 128), F32), vm((2, 8, 128), F32),
        pltpu.SemaphoreType.DMA((12,)), pltpu.SemaphoreType.DMA((NSEM,)), pltpu.SemaphoreType.DMA((NSEM,)),
    ]
    return pl.pallas_call(
        kernel,
        out_shape=pltpu.VMEM((HALF, R), F32),
        in_specs=[pl.BlockSpec(memory_space=pltpu.HBM)] * 2,
        out_specs=pl.BlockSpec(memory_space=pltpu.VMEM),
        scratch_shapes=scratch,
        name="cp_step",
        cost_estimate=pl.CostEstimate(flops=10**10, bytes_accessed=10**7, transcendentals=0),
        compiler_params=pltpu.CompilerParams(
            collective_id=0, has_side_effects=True, vmem_limit_bytes=50 * 2**20
        ),
    )(samples, factor)


def solution(mesh):
    placed = (P("samples", "feat"), P("feat", None))
    return jax.shard_map(
        per_device, mesh=mesh, in_specs=placed, out_specs=P("feat", None), check_vma=False
    )
```

```python
import jax
import jax.numpy as jnp
from jax import lax
from jax.experimental import pallas as pl
from jax.experimental.pallas import tpu as pltpu
from jax.sharding import PartitionSpec as P

D = 4096
R = 512
NROWS = 32768
HALF = D // 2
ROWS = 256
COLS = 256
DEPTH = 512
MINE = HALF // 2
MESH = pl.DeviceIdType.MESH
F32 = jnp.float32
BF16 = jnp.bfloat16

STREAMS = ((1, 0, 4), (-1, 1, 4), (1, 1, 3), (-1, 0, 3))
SLOT = {}
for _k in range(1, 5):
    for _i, (_, _, _hops) in enumerate(STREAMS):
        if _k <= _hops:
            SLOT[(_i, _k)] = len(SLOT)
NSLOT = len(SLOT)


def split(v):
    hi = v.astype(BF16)
    return hi, (v - hi.astype(F32)).astype(BF16)


def dot3(ah, al, bh, bl, dims=(((1,), (0,)), ((), ()))):
    def one(a, b):
        return lax.dot_general(a, b, dims, preferred_element_type=F32)

    return one(ah, bh) + (one(ah, bl) + one(al, bh))


def kernel(
    x_hbm, f_hbm, o_ref,
    xv, xo, fv, fh, fl, xh, xl, p, pr, s, so, xth, xtl, mom,
    ring, acc_a, dir_a, yrecv, acc_b, zrecv, acc_b2, xrecv,
    gram, gram_mine, gram_other, wh, wl, grad, ss1, ss2, ss3, ss4,
    load_sem, send, recv,
):
    sidx = lax.axis_index("samples")
    feat = lax.axis_index("feat")
    core = lax.rem(sidx, 2)
    z = lax.rem(sidx // 2, 8)
    y = lax.rem(sidx // 16, 4)
    xhi = sidx // 64

    def dev(a, b, c, d, e):
        return (((a * 4 + b) * 8 + c) * 2 + d, e)

    other = dev(xhi, y, z, 1 - core, feat)
    partner = dev(xhi, y, z, core, 1 - feat)

    def yx_of(j):
        return lax.rem(y + j // 2, 4), lax.rem(xhi + j % 2, 2)

    def yx_peer(j):
        a, b = yx_of(j)
        return dev(b, a, z, core, feat)

    def y_of(j):
        return lax.rem(y + j + 4, 4)

    def y_peer(j):
        return dev(xhi, y_of(j), z, core, feat)

    def z_of(j):
        return lax.rem(z + j + 8, 8)

    def z_peer(j):
        return dev(xhi, y, z_of(j), core, feat)

    def span(at, n):
        return pl.ds(pl.multiple_of(at, 16), n)

    counter = [0]
    unsent = []

    def start(src, dst, to):
        i = counter[0]
        counter[0] += 1
        c = pltpu.make_async_remote_copy(
            src_ref=src, dst_ref=dst, send_sem=send.at[i], recv_sem=recv.at[i],
            device_id=to, device_id_type=MESH,
        )
        c.start()
        unsent.append(c)
        return c

    barrier = pltpu.get_barrier_semaphore()
    everyone = [other, partner] + [yx_peer(j) for j in range(1, 8)] + [z_peer(j) for j in range(1, 8)]
    for to in everyone:
        pl.semaphore_signal(barrier, inc=1, device_id=to, device_id_type=MESH)

    def kspan(k):
        return pl.ds(k * DEPTH, DEPTH)

    load_x = [pltpu.make_async_copy(x_hbm.at[:, kspan(k)], xv.at[:, kspan(k)], load_sem.at[k]) for k in range(4)]
    load_f = [
        [
            pltpu.make_async_copy(
                f_hbm.at[kspan(k), pl.ds(h * COLS, COLS)], fv.at[h, kspan(k), :], load_sem.at[4 + 4 * h + k]
            )
            for k in range(4)
        ]
        for h in range(2)
    ]
    for k in range(4):
        load_x[k].start()
        load_f[0][k].start()
    for k in range(4):
        load_f[1][k].start()
    def split_factor(h, k):
        load_f[h][k].wait()

        def body(i, _):
            r = pl.ds(pl.multiple_of(k * DEPTH + i * 128, 128), 128)
            fh[h, r, :], fl[h, r, :] = split(fv[h, r, :])
            return 0

        lax.fori_loop(0, DEPTH // 128, body, 0)

    def project(h):
        for k in range(4):
            if h == 0:
                load_x[k].wait()

                def split_x(i, _):
                    r = pl.ds(pl.multiple_of(i * 64, 64), 64)
                    xh[r, kspan(k)], xl[r, kspan(k)] = split(xv[r, kspan(k)])
                    return 0

                lax.fori_loop(0, ROWS // 64, split_x, 0)
            if h == 0:
                split_factor(0, k)
            part = dot3(xh[:, kspan(k)], xl[:, kspan(k)], fh[h, kspan(k), :], fl[h, kspan(k), :])
            for i in range(2):
                piece = part[:, i * 128 : (i + 1) * 128]
                p[2 * h + i] = piece if k == 0 else p[2 * h + i] + piece

    proj_copy = {}

    def exchange(q):
        proj_copy[q] = start(p.at[q], pr.at[q], partner)

    project(0)
    pl.semaphore_wait(barrier, len(everyone))
    exchange(0)
    for k in range(4):
        split_factor(1, k)
    exchange(1)

    contract = (((0,), (0,)), ((), ()))
    chip = (xhi * 4 + y) * 8 + z
    block = chip // 16
    block_at = pl.ds(pl.multiple_of(lax.rem(block, 2) * 128, 128), 128)
    block_half = block // 2
    eight = pl.ds(pl.multiple_of(lax.rem(chip, 16) * 8, 8), 8)
    for h in range(2):
        cols = slice(h * COLS, (h + 1) * COLS)
        for k in range(4):
            part = dot3(
                fh[block_half, kspan(k), block_at], fl[block_half, kspan(k), block_at],
                fh[h, kspan(k), :], fl[h, kspan(k), :], contract,
            )
            gram[:, cols] = part if k == 0 else gram[:, cols] + part
    gram_mine[...] = gram[eight, :]
    g_copy = start(gram_mine, gram_other, partner)
    x_copy = start(x_hbm.at[:, pl.ds(pl.multiple_of((1 - core) * MINE, MINE), MINE)], xo, other)

    project(1)
    exchange(2)

    def turn(src, base, at):
        def body(i, _):
            c = pl.ds(pl.multiple_of(base + i * 128, 128), 128)
            r = pl.ds(pl.multiple_of(i * 128, 128), 128)
            hi, lo = split(src[:, c].T)
            xth[r, at : at + ROWS] = hi
            xtl[r, at : at + ROWS] = lo
            return 0

        lax.fori_loop(0, MINE // 128, body, 0)

    turn(xv, core * MINE, 0)
    exchange(3)
    x_copy.wait_recv()
    turn(xo, 0, ROWS)

    base = core * MINE
    s_copy = {}

    def squares(q):
        proj_copy[q].wait_recv()
        total = p[q] + pr[q]
        s[q] = total * total
        s_copy[q] = start(s.at[q], so.at[q], other)

    def stacked(q):
        s_copy[q].wait_recv()
        ah, al = split(s[q])
        bh, bl = split(so[q])
        return jnp.concatenate([ah, bh], axis=0), jnp.concatenate([al, bl], axis=0)

    def moment(q, sh, sl, at, n):
        r = pl.ds(pl.multiple_of(at, n), n)
        w = pl.ds(pl.multiple_of(base + at, n), n)
        cols = slice(q * 128, (q + 1) * 128)
        mom[q, r, :] = dot3(xth[r, :], xtl[r, :], sh, sl) - dot3(
            fh[block_half, w, block_at], fl[block_half, w, block_at], wh[:, cols], wl[:, cols]
        )

    y_copy, xb_copy, zb_copy = {}, {}, {}

    def y_start(q):
        sh, sl = stacked(q)
        for j in (2, 1, 3):
            moment(q, sh, sl, y_of(j) * 256, 256)
            y_copy[(j, q)] = start(
                mom.at[q, pl.ds(pl.multiple_of(y_of(j) * 256, 256), 256), :], yrecv.at[q // 2, j - 1], y_peer(j)
            )
        moment(q, sh, sl, y * 256, 256)

    def y_sum(q):
        for j in (1, 3, 2):
            y_copy[(j, q)].wait_recv()
        i = q // 2
        mine = mom[q, pl.ds(pl.multiple_of(y * 256, 256), 256), :]
        acc_b[i] = (mine + yrecv[i, 0]) + (yrecv[i, 1] + yrecv[i, 2])
        xb_copy[q] = start(acc_b.at[i, pl.ds(pl.multiple_of((1 - xhi) * 128, 128), 128), :], xrecv.at[i], yx_peer(1))

    def x_sum(q):
        i = q // 2
        xb_copy[q].wait_recv()
        acc_b2[i] = acc_b[i, pl.ds(pl.multiple_of(xhi * 128, 128), 128), :] + xrecv[i]
        for j in (4, 3, 5, 2, 6, 1, 7):
            zb_copy[(j, q)] = start(acc_b2.at[i, span(z_of(j) * 16, 16), :], zrecv.at[i, j - 1], z_peer(j))

    def z_sum(q):
        i = q // 2
        part = acc_b2[i, span(z * 16, 16), :]
        for j in range(1, 8):
            zb_copy[(j, q)].wait_recv()
        for j in range(1, 8):
            part = part + zrecv[i, j - 1]
        return part

    def zrows(zz, half):
        return pl.ds(pl.multiple_of(zz * 128 + half * 64, 64), 64)

    ring_copy, da_copy = {}, {}

    def ring_hop(q, i, k):
        way, half, hops = STREAMS[i]
        if k > hops:
            return
        r = zrows(z_of(way * (hops + 1 - k)), half)
        if k > 1:
            ring_copy[(q, i, k - 1)].wait_recv()
            mom[q, r, :] += ring[q // 2, SLOT[(i, k - 1)]]
        ring_copy[(q, i, k)] = start(mom.at[q, r, :], ring.at[q // 2, SLOT[(i, k)]], z_peer(way))

    def ring_step(q, k):
        for i in range(4):
            ring_hop(q, i, k)

    def ring_start(q):
        sh, sl = stacked(q)
        moment(q, sh, sl, z_of(4) * 128, 128)
        ring_hop(q, 0, 1)
        ring_hop(q, 1, 1)
        moment(q, sh, sl, z_of(3) * 128, 128)
        ring_hop(q, 2, 1)
        moment(q, sh, sl, z_of(-3) * 128, 128)
        ring_hop(q, 3, 1)
        for j in (2, -2, 1, -1, 0):
            moment(q, sh, sl, z_of(j) * 128, 128)

    def ring_end(q):
        for half in range(2):
            parts = []
            for i, (way, h, hops) in enumerate(STREAMS):
                if h == half:
                    ring_copy[(q, i, hops)].wait_recv()
                    parts.append(ring[q // 2, SLOT[(i, hops)]])
            acc_a[q // 2, half * 64 : half * 64 + 64, :] = mom[q, zrows(z, half), :] + (parts[0] + parts[1])
        for j in (5, 4, 1, 3, 7, 2, 6):
            a, b = yx_of(j)
            da_copy[(j, q)] = start(acc_a.at[q // 2, span(a * 32 + b * 16, 16), :], dir_a.at[q // 2, j - 1], yx_peer(j))

    def direct_sum(q):
        part = acc_a[q // 2, span(y * 32 + xhi * 16, 16), :]
        for j in range(1, 8):
            da_copy[(j, q)].wait_recv()
        for j in range(1, 8):
            part = part + dir_a[q // 2, j - 1]
        return part

    def gram_weights():
        gram[...] = jnp.zeros_like(gram)
        g_copy.wait_recv()
        whole = (gram_mine[...] + gram_other[...]) * (1.0 / D)
        gram[eight, :] = whole * whole * (NROWS * D / 64.0)
        wh[...], wl[...] = split(gram[...])

    row = (y * 256 + xhi * 128 + z * 16, z * 128 + y * 32 + xhi * 16)

    squares_of = []

    def finish(q, total):
        gq = total * (-6.0 / 64.0 / (NROWS * D))
        squares_of.append(gq * gq)
        grad[q, span(base + row[1 - q % 2], 16), :] = gq

    forward = []
    waiting = []
    rate = []
    zg_copy, xg_copy, yg_copy, aa_copy, gather = {}, {}, {}, {}, {}

    def update(q, at, n):
        r = span(at, n)
        c = (q % 2) * 128
        o_ref[r, q * 128 : (q + 1) * 128] = fv[q // 2, r, c : c + 128] - grad[q, r, :] * rate[0]

    def send_rows(q, at, n, to):
        r = span(base + at, n)
        return start(grad.at[q, r, :], grad.at[q, r, :], to)

    def arrived(q, at, n):
        forward.append((send_rows(q, at, n, other), q, at, n))
        if rate:
            update(q, base + at, n)
        else:
            waiting.append((q, at, n))

    def own_y(q):
        finish(q, z_sum(q))
        zg_copy[q] = [send_rows(q, row[0], 16, z_peer(j)) for j in (4, 3, 5, 2, 6, 1, 7)]

    def own_ring(q):
        finish(q, direct_sum(q))
        aa_copy[q] = [send_rows(q, row[1], 16, yx_peer(j)) for j in (5, 4, 1, 3, 7, 2, 6)]

    def y_rows(yy, i):
        return yy * 256 + (xhi * 128 if i == 0 else (1 - xhi) * 128)

    def y_spread(q, i):
        at = y_rows(y, i)
        if i == 0:
            for c in zg_copy[q]:
                c.wait_recv()
            xg_copy[q] = send_rows(q, at, 128, yx_peer(1))
        else:
            xg_copy[q].wait_recv()
        for j in (2, 1, 3):
            yg_copy[(q, i, j)] = send_rows(q, at, 128, y_peer(j))
        arrived(q, at, 128)

    def y_land(q, i):
        for j in (1, 3, 2):
            yg_copy[(q, i, j)].wait_recv()
            arrived(q, y_rows(y_of(-j), i), 128)

    def gather_step(q, k):
        if k == 1:
            for c in aa_copy[q]:
                c.wait_recv()
        for i, (way, half, hops) in enumerate(STREAMS):
            if k > hops + 1:
                continue
            at = z_of(-way * (k - 1)) * 128 + half * 64
            if k > 1:
                gather[(q, i, k - 1)].wait_recv()
            if k <= hops:
                gather[(q, i, k)] = send_rows(q, at, 64, z_peer(way))
            if k > 1:
                arrived(q, at, 64)
        if k == 1:
            arrived(q, z * 128, 128)

    done = []

    def from_other(upto):
        while len(done) < upto:
            c, q, at, n = forward[len(done)]
            c.wait_recv()
            update(q, (1 - core) * MINE + at, n)
            done.append(0)

    squares(0)
    gram_weights()
    ring_start(0)
    squares(1)
    y_start(1)
    squares(2)
    ring_step(0, 2)
    ring_start(2)
    squares(3)
    ring_step(0, 3)
    y_start(3)
    ring_step(2, 2)
    ring_step(0, 4)
    y_sum(1)
    ring_step(2, 3)
    ring_end(0)
    x_sum(1)
    ring_step(2, 4)
    y_sum(3)
    own_ring(0)
    own_y(1)
    ring_end(2)
    x_sum(3)
    gather_step(0, 1)
    y_spread(1, 0)
    own_ring(2)
    own_y(3)
    sq = (squares_of[0] + squares_of[1]) + (squares_of[2] + squares_of[3])
    me1 = y * 2 + xhi
    ss1[me1] = sq[0:8] + sq[8:16]
    s1_copy = [start(ss1.at[me1], ss1.at[me1], yx_peer(j)) for j in range(1, 8)]
    y_spread(1, 1)
    gather_step(0, 2)
    for c in s1_copy:
        c.wait_recv()
    tile = ss1[0]
    for j in range(1, 8):
        tile = tile + ss1[j]
    ss2[z] = tile
    s2_copy = [start(ss2.at[z], ss2.at[z], z_peer(j)) for j in range(1, 8)]
    gather_step(2, 1)
    y_spread(3, 0)
    gather_step(0, 3)
    y_spread(3, 1)
    gather_step(2, 2)
    gather_step(0, 4)
    for c in s2_copy:
        c.wait_recv()
    tile = ss2[0]
    for j in range(1, 8):
        tile = tile + ss2[j]
    ss3[core] = tile
    s3_copy = start(ss3.at[core], ss3.at[core], other)
    s3_copy.wait_recv()
    ss4[feat] = ss3[0] + ss3[1]
    s4_copy = start(ss4.at[feat], ss4.at[feat], partner)
    gather_step(2, 3)
    y_land(1, 0)
    gather_step(0, 5)
    y_land(1, 1)
    s4_copy.wait_recv()
    total = jnp.sum(ss4[0] + ss4[1], keepdims=True)
    rms = jnp.sqrt(total * (1.0 / (D * R))) + 1e-06
    rate.append(0.5 / rms)
    for q, at, n in waiting:
        update(q, base + at, n)
    y_land(3, 0)
    gather_step(2, 4)
    from_other(len(forward) - 8)
    y_land(3, 1)
    gather_step(2, 5)
    from_other(len(forward))
    for c in unsent:
        c.wait_send()


NSEM = 256


def per_device(samples, factor):
    vm = pltpu.VMEM
    scratch = [
        vm((ROWS, HALF), F32), vm((ROWS, MINE), F32), vm((2, HALF, COLS), F32),
        vm((2, HALF, COLS), BF16), vm((2, HALF, COLS), BF16),
        vm((ROWS, HALF), BF16), vm((ROWS, HALF), BF16),
        vm((4, ROWS, 128), F32), vm((4, ROWS, 128), F32), vm((4, ROWS, 128), F32), vm((4, ROWS, 128), F32),
        vm((MINE, 2 * ROWS), BF16), vm((MINE, 2 * ROWS), BF16), vm((4, MINE, 128), F32),
        vm((2, NSLOT, 64, 128), F32), vm((2, 128, 128), F32), vm((2, 7, 16, 128), F32),
        vm((2, 3, 256, 128), F32), vm((2, 256, 128), F32), vm((2, 7, 16, 128), F32),
        vm((2, 128, 128), F32), vm((2, 128, 128), F32),
        vm((128, R), F32), vm((8, R), F32), vm((8, R), F32), vm((128, R), BF16), vm((128, R), BF16),
        vm((4, HALF, 128), F32),
        vm((8, 8, 128), F32), vm((8, 8, 128), F32), vm((2, 8, 128), F32), vm((2, 8, 128), F32),
        pltpu.SemaphoreType.DMA((12,)), pltpu.SemaphoreType.DMA((NSEM,)), pltpu.SemaphoreType.DMA((NSEM,)),
    ]
    return pl.pallas_call(
        kernel,
        out_shape=pltpu.VMEM((HALF, R), F32),
        in_specs=[pl.BlockSpec(memory_space=pltpu.HBM)] * 2,
        out_specs=pl.BlockSpec(memory_space=pltpu.VMEM),
        scratch_shapes=scratch,
        name="cp_step",
        cost_estimate=pl.CostEstimate(flops=10**10, bytes_accessed=10**7, transcendentals=0),
        compiler_params=pltpu.CompilerParams(
            collective_id=0, has_side_effects=True, vmem_limit_bytes=50 * 2**20
        ),
    )(samples, factor)


def solution(mesh):
    placed = (P("samples", "feat"), P("feat", None))
    return jax.shard_map(
        per_device, mesh=mesh, in_specs=placed, out_specs=P("feat", None), check_vma=False
    )
```
